768 devices in a mesh: dp: 24 (over x_hi, z), expert: 32 (over y, x_lo, core).
Axes of the slice: x: 4 (x_hi: 2, x_lo: 2; x = x_hi * 2 + x_lo), y: 8, z: 12, core: 2. Of those that a mesh axis runs over, the one named last changes fastest.
Arguments:
- token_rows: bfloat16 [49152, 4096], P(('dp', 'expert')), may hold values from -6 to 6
- row_scales: bfloat16 [49152], P(('dp', 'expert')), may hold values from 0.099609375 to 2
- expert_ids: int32 [49152, 8], P(('dp', 'expert')), may hold values from 0 to 127, all different within a row; in each aligned block of 64 rows (0 to 63, 64 to 127, ...) at most 5 rows name the same one
- gate_values: bfloat16 [49152, 8], P(('dp', 'expert')), may hold values from 0.049804688 to 0.59765625
- upstream: bfloat16 [49152, 8, 768], P(('dp', 'expert')), may hold values from -6 to 6
- weight: bfloat16 [32, 4096, 768], P('expert'), may hold values from -0.09375 to 0.09375
Outputs:
- token_grads: bfloat16 [49152, 4096], P(('dp', 'expert'))
- gate_grads: bfloat16 [49152, 8], P(('dp', 'expert'))
- weight_grads: float32 [32, 4096, 768], P('expert', None, 'dp')
The draws below stay inside these ranges and needn't reach their ends.
Inputs may be any that keep to these rules, and one draw needn't show every extreme that they name: `expert_ids`: each row names 8 different experts; among the 64 rows of one device no expert is named more than 5 times.
All inputs are finite; a program needn't handle non-finite values.
Results may differ from the reference program's by a relative error of at most 0.02.
Values may be sent and summed in bfloat16 or wider, within the bound.
No kernel may reach another device: no remote copies, remote signals or barrier semaphores. Data moves between devices by JAX's collectives and lax.ppermute only.
A program may use at most 64 MiB of HBM per device.

```python
import math
import jax
import jax.numpy as jnp
import numpy as np
from jax import lax

D = 4096
F = 768
EXPERTS = 128
TOP = 8
TOK_DEV = 64
CAP = 5
EXP_WIN = 32
TOKENS = 49152
N_DP = 24
N_EXPERT = 32


def steps_of(key, shape, pieces, least, top_value):
    factor_of, own = 1.0, jax.random.fold_in(key, 6)
    for dim, parts in pieces:
        steps = jnp.exp(jax.random.uniform(jax.random.fold_in(own, dim), (parts,), jnp.float32, least / len(pieces), top_value / len(pieces)))
        factor_of = factor_of * jnp.repeat(steps, shape[dim] // parts).reshape([-1 if axis == dim else 1 for axis in range(len(shape))])
    return factor_of


def shared_out(rng, own, number, rows, number_of, top, bound, skew):
    order = jax.random.permutation(rng, number_of)
    packed, usual = portions_of(number_of, rows * top, bound, skew, True), portions_of(number_of, rows * top, bound, skew, False)
    places = jnp.arange(number_of)

    def named(sizes, offset_by):
        used = int((sizes > 0).sum())
        fixed = max(1, used // 4)
        passed = fixed + (places - fixed + offset_by * (used - fixed)) % max(1, number_of - fixed)
        return jnp.zeros((number_of,), jnp.int32).at[order[jnp.where(places < fixed, places, passed)]].set(jnp.asarray(sizes, jnp.int32))

    sizes = jnp.where(number % 4 == 0, named(packed, number // 4), named(usual, number - number // 4 - 1))
    mixed = jax.random.permutation(jax.random.fold_in(own, 3), number_of)
    source_of, taker = mixed[0:number_of // 2 * 2:2], mixed[1:number_of // 2 * 2:2]
    room = jnp.minimum(sizes[source_of] - 1, bound - sizes[taker]) // 2
    room = jnp.where((source_of == order[0]) | (taker == order[0]) | (sizes[taker] == 0), 0, jnp.maximum(room, 0))
    passed = jax.random.randint(jax.random.fold_in(own, 4), (number_of // 2,), 0, 1 << 20) % (room + 1)
    sizes = sizes.at[source_of].add(-passed).at[taker].add(passed)
    items = jnp.searchsorted(jnp.cumsum(sizes), jnp.arange(rows * top), side="right").astype(jnp.int32)
    grid = items.reshape(top, rows).T
    grid = grid[jax.random.permutation(jax.random.fold_in(own, 1), rows)]
    offset_by = jax.random.randint(jax.random.fold_in(own, 2), (rows, 1), 0, top)
    return jnp.take_along_axis(grid, (jnp.arange(top)[None, :] + offset_by) % top, axis=1)


def portions_of(count, total, bound, skew, full):
    portions = [(1 << 20) // math.isqrt(rank ** skew) + 1 for rank in range(1, count + 1)]
    largest = bound if full else min(bound, max(-(-total // count), total * portions[0] // sum(portions)))
    least = 1 if total - largest >= count - 1 else 0
    given, spare = [largest] + [least] * (count - 1), total - largest - least * (count - 1)
    while spare > 0:
        candidates = [i for i in range(1, count) if given[i] < largest] or [i for i in range(1, count) if given[i] < bound]
        whole, budget = sum([portions[i] for i in candidates]), spare
        for i in candidates:
            more = min(bound - given[i], max(1, budget * portions[i] // whole), spare)
            given[i] = given[i] + more
            spare = spare - more
    return np.array(given)


def bell_draw(key, dims, scale, bound, split=(), kind=jnp.bfloat16):
    array = scale * jax.random.normal(key, dims, jnp.float32)
    if split:
        array = array * steps_of(key, dims, split, -0.22, 0.18)
    return jnp.clip(array, -bound, bound).astype(kind)


def setup_inputs(seed: int = 0) -> dict:
    streams_of = jax.random.split(jax.random.key(seed), 7)
    token_rows = bell_draw(streams_of[0], (TOKENS, D), 1.0, 6.0, ((0, 768),))
    row_scales = jnp.clip(jnp.exp(math.log(2.0) - 2.9996462 * jax.random.uniform(streams_of[1], (TOKENS,), jnp.float32) ** steps_of(streams_of[1], (TOKENS,), ((0, 768),), -0.2, 0.2)), 0.099609375, 2.0).astype(jnp.bfloat16)
    expert_ids_keys = jax.random.split(jax.random.fold_in(streams_of[2], 1), TOKENS // TOK_DEV)
    expert_ids_turns = jax.random.permutation(jax.random.fold_in(streams_of[2], 3), TOKENS // TOK_DEV)
    expert_ids = jax.vmap(lambda own, number: shared_out(jax.random.fold_in(streams_of[2], 2), own, number, TOK_DEV, EXPERTS, TOP, CAP, 2))(expert_ids_keys, expert_ids_turns).reshape((TOKENS, TOP))
    gate_values = jnp.clip(0.049804688 + 0.54785156 * jax.random.uniform(streams_of[3], (TOKENS, TOP), jnp.float32) ** steps_of(streams_of[3], (TOKENS, TOP), ((0, 768),), -0.2, 0.2), 0.049804688, 0.59765625).astype(jnp.bfloat16)
    upstream = bell_draw(streams_of[4], (TOKENS, TOP, F), 1.0, 6.0, ((0, 768),))
    weight = bell_draw(streams_of[5], (EXP_WIN, D, F), D ** -0.5, 0.09375, ((0, 32),))
    return dict(token_rows=token_rows, row_scales=row_scales, expert_ids=expert_ids, gate_values=gate_values, upstream=upstream, weight=weight)


def expert_work(operands):
    packed_rows, packed_up, packed_gate, matrix = operands
    slots = packed_rows.shape[0] * packed_rows.shape[1]
    rows_flat = packed_rows.reshape(slots, D)
    up_flat = packed_up.reshape(slots, F)
    gate_flat = packed_gate.reshape(slots)
    out_grad = (gate_flat.astype(jnp.float32)[:, None] * up_flat.astype(jnp.float32)).astype(jnp.bfloat16)
    recomputed = jnp.dot(rows_flat, matrix, preferred_element_type=jnp.float32)
    gate_terms = jnp.sum(up_flat.astype(jnp.float32) * recomputed, axis=1).astype(jnp.bfloat16)
    row_grads = jnp.dot(out_grad, matrix.T, preferred_element_type=jnp.float32).astype(jnp.bfloat16)
    partial_grad = jnp.dot(rows_flat.T, out_grad, preferred_element_type=jnp.float32).astype(jnp.bfloat16)
    return (row_grads.reshape(packed_rows.shape), gate_terms.reshape(packed_gate.shape), partial_grad)


def reference(token_rows, row_scales, expert_ids, gate_values, upstream, weight):
    sources = N_EXPERT
    replicas = N_DP
    rows_all = token_rows.reshape(replicas, sources, TOK_DEV, D)
    scales_all = row_scales.reshape(replicas, sources, TOK_DEV)
    ids_all = expert_ids.reshape(replicas, sources, TOK_DEV, TOP)
    gates_all = gate_values.reshape(replicas, sources, TOK_DEV, TOP)
    up_all = upstream.reshape(replicas, sources, TOK_DEV, TOP, F)

    def replica(total, inputs):
        rows_here, scales_here, ids_here, gates_here, up_here = inputs
        dequant = (scales_here.astype(jnp.float32)[..., None] * rows_here.astype(jnp.float32)).astype(jnp.bfloat16)
        onehot = (ids_here[..., None] == jnp.arange(EXP_WIN, dtype=jnp.int32)).astype(jnp.int32)
        onehot = onehot.reshape(sources, TOK_DEV * TOP, EXP_WIN)
        before = jnp.cumsum(onehot, axis=1) - onehot
        slot_index = jnp.sum(before * onehot, axis=2).reshape(sources, TOK_DEV, TOP).astype(jnp.int32)
        source_index = jnp.broadcast_to(jnp.arange(sources, dtype=jnp.int32)[:, None, None], ids_here.shape)
        row_picks = jnp.broadcast_to(dequant[:, :, None, :], (sources, TOK_DEV, TOP, D))
        packed_rows = jnp.zeros((EXP_WIN, sources, CAP, D), jnp.bfloat16).at[ids_here, source_index, slot_index].set(row_picks, mode="drop")
        packed_up = jnp.zeros((EXP_WIN, sources, CAP, F), jnp.bfloat16).at[ids_here, source_index, slot_index].set(up_here, mode="drop")
        packed_gate = jnp.zeros((EXP_WIN, sources, CAP), jnp.bfloat16).at[ids_here, source_index, slot_index].set(gates_here, mode="drop")
        row_grads, gate_terms, partial_grad = lax.map(expert_work, (packed_rows, packed_up, packed_gate, weight))
        picked = row_grads.at[ids_here, source_index, slot_index].get(mode="fill", fill_value=0)
        token_grad = jnp.sum(picked.astype(jnp.float32), axis=2).astype(jnp.bfloat16)
        gate_grad = gate_terms.at[ids_here, source_index, slot_index].get(mode="fill", fill_value=0)
        return total + partial_grad.astype(jnp.float32), (token_grad, gate_grad)

    start = jnp.zeros((EXP_WIN, D, F), jnp.float32)
    weight_grads, (token_grads, gate_grads) = lax.scan(replica, start, (rows_all, scales_all, ids_all, gates_all, up_all))
    return (token_grads.reshape(TOKENS, D), gate_grads.reshape(TOKENS, TOP), weight_grads)
```

```python
import jax
import jax.numpy as jnp
from jax import lax
from jax.sharding import Mesh, PartitionSpec as P

CAP = 5
LANE = 128
EXPERT_AXES = ("y", "xl", "c")
ALL_AXES = ("xh", "z") + EXPERT_AXES


def dot_t(a, b):
    return lax.dot_general(a, b, (((0,), (0,)), ((), ())), preferred_element_type=jnp.float32)


def local(token_rows, row_scales, expert_ids, gate_values, upstream, weight):
    toks, picks = expert_ids.shape
    width = token_rows.shape[1]
    hidden = upstream.shape[2]
    experts = lax.axis_size(EXPERT_AXES)
    slots = experts * CAP
    choices = toks * picks
    half = hidden // 2
    x_lines = CAP * width // LANE
    dz_lines = CAP * hidden // LANE

    x = (row_scales.astype(jnp.float32)[:, None] * token_rows.astype(jnp.float32)).astype(
        jnp.bfloat16
    )
    dz = (gate_values.astype(jnp.float32)[..., None] * upstream.astype(jnp.float32)).astype(
        jnp.bfloat16
    )
    ids = expert_ids.reshape(choices)
    onehot = (ids[:, None] == jnp.arange(experts, dtype=jnp.int32)[None, :]).astype(jnp.int32)
    before = jnp.cumsum(onehot, axis=0) - onehot
    slot = jnp.sum(before * onehot, axis=1)
    position = jnp.where(ids < experts, ids * CAP + slot, -1)
    placing = position[:, None] == jnp.arange(slots, dtype=jnp.int32)[None, :]
    place = placing.astype(jnp.bfloat16)
    token_place = jnp.sum(
        placing.astype(jnp.int32).reshape(toks, picks, slots), axis=1
    ).astype(jnp.bfloat16)

    send_x = dot_t(token_place, x).astype(jnp.bfloat16)
    send_dz = dot_t(place, dz.reshape(choices, hidden)).astype(jnp.bfloat16)
    pad = (-(x_lines + dz_lines)) % 16
    message = jnp.concatenate(
        [
            send_x.reshape(experts, x_lines, LANE),
            send_dz.reshape(experts, dz_lines, LANE),
            jnp.zeros((experts, pad, LANE), jnp.bfloat16),
        ],
        axis=1,
    )
    mine = lax.all_to_all(message, EXPERT_AXES, 0, 0, tiled=True)
    other = lax.ppermute(mine, "xh", [(0, 1), (1, 0)])

    def unpack(raw):
        rows = raw[:, :x_lines].reshape(slots, width)
        grads = raw[:, x_lines : x_lines + dz_lines].reshape(slots, hidden)
        return rows, grads

    x_in, dz_in = unpack(mine)
    matrix = weight[0]
    row_grads = lax.dot_general(
        dz_in, matrix, (((1,), (1,)), ((), ())), preferred_element_type=jnp.float32
    ).astype(jnp.bfloat16)
    z = jnp.dot(x_in, matrix, preferred_element_type=jnp.float32)
    terms = jnp.sum(dz_in.astype(jnp.float32) * z, axis=1).astype(jnp.bfloat16)
    reply = jnp.concatenate(
        [
            row_grads.reshape(experts, x_lines, LANE),
            jnp.pad(terms.reshape(experts, 1, CAP), ((0, 0), (0, 15), (0, LANE - CAP))),
        ],
        axis=1,
    )
    back = lax.all_to_all(reply, EXPERT_AXES, 0, 0, tiled=True)

    x_other, dz_other = unpack(other)
    at = lax.axis_index("xh") * half
    x_both = jnp.concatenate([x_in, x_other], axis=0)
    dz_both = jnp.concatenate(
        [
            lax.dynamic_slice_in_dim(dz_in, at, half, 1),
            lax.dynamic_slice_in_dim(dz_other, at, half, 1),
        ],
        axis=0,
    )
    partial = dot_t(dz_both, x_both).astype(jnp.bfloat16)
    weight_grads = lax.psum_scatter(partial, "z", scatter_dimension=0, tiled=True)

    back_rows = back[:, :x_lines].reshape(slots, width)
    back_terms = back[:, x_lines, :CAP].reshape(slots).astype(jnp.float32)
    token_grads = jnp.dot(token_place, back_rows, preferred_element_type=jnp.float32).astype(
        jnp.bfloat16
    )
    picked = jnp.sum(jnp.where(placing, back_terms[None, :], 0.0), axis=1)
    gate_grads = (picked.reshape(toks, picks) / gate_values.astype(jnp.float32)).astype(
        jnp.bfloat16
    )
    return token_grads, gate_grads, weight_grads.astype(jnp.float32).T[None]


def solution(mesh):
    n_dp, n_expert = mesh.shape["dp"], mesh.shape["expert"]
    fine = Mesh(mesh.devices.reshape(2, n_dp // 2, n_expert // 4, 2, 2), ALL_AXES)
    rows = P(ALL_AXES)
    in_specs = (rows, rows, rows, rows, rows, P(EXPERT_AXES))
    out_specs = (rows, rows, P(EXPERT_AXES, None, ("xh", "z")))
    return jax.shard_map(
        local, mesh=fine, in_specs=in_specs, out_specs=out_specs, check_vma=False
    )
```

```python
import jax
import jax.numpy as jnp
from jax import lax
from jax.sharding import Mesh, PartitionSpec as P

CAP = 5
LANE = 128
EXPERT_AXES = ("y", "xl", "c")
ALL_AXES = ("xh", "z") + EXPERT_AXES


def dot_t(a, b):
    return lax.dot_general(a, b, (((0,), (0,)), ((), ())), preferred_element_type=jnp.float32)


def local(token_rows, row_scales, expert_ids, gate_values, upstream, weight):
    toks, picks = expert_ids.shape
    width = token_rows.shape[1]
    hidden = upstream.shape[2]
    experts = lax.axis_size(EXPERT_AXES)
    depth = lax.axis_size("z")
    slots = experts * CAP
    choices = toks * picks
    half = hidden // 2
    x_lines = CAP * width // LANE
    dz_lines = CAP * hidden // LANE

    x = (row_scales.astype(jnp.float32)[:, None] * token_rows.astype(jnp.float32)).astype(
        jnp.bfloat16
    )
    dz = (gate_values.astype(jnp.float32)[..., None] * upstream.astype(jnp.float32)).astype(
        jnp.bfloat16
    )
    ids = expert_ids.reshape(choices)
    onehot = (ids[:, None] == jnp.arange(experts, dtype=jnp.int32)[None, :]).astype(jnp.int32)
    before = jnp.cumsum(onehot, axis=0) - onehot
    slot = jnp.sum(before * onehot, axis=1)
    position = jnp.where(ids < experts, ids * CAP + slot, -1)
    placing = position[:, None] == jnp.arange(slots, dtype=jnp.int32)[None, :]
    place = placing.astype(jnp.bfloat16)
    token_place = jnp.sum(
        placing.astype(jnp.int32).reshape(toks, picks, slots), axis=1
    ).astype(jnp.bfloat16)

    send_x = dot_t(token_place, x).astype(jnp.bfloat16)
    send_dz = dot_t(place, dz.reshape(choices, hidden)).astype(jnp.bfloat16)
    pad = (-(x_lines + dz_lines)) % 16
    message = jnp.concatenate(
        [
            send_x.reshape(experts, x_lines, LANE),
            send_dz.reshape(experts, dz_lines, LANE),
            jnp.zeros((experts, pad, LANE), jnp.bfloat16),
        ],
        axis=1,
    )
    mine = lax.all_to_all(message, EXPERT_AXES, 0, 0, tiled=True)
    x_in = mine[:, :x_lines].reshape(slots, width)
    dz_in = mine[:, x_lines : x_lines + dz_lines].reshape(slots, hidden)

    unit = jnp.arange(hidden)
    shard = hidden // (2 * depth)
    source = (unit // shard % 2) * half + unit // (2 * shard) * shard + unit % shard
    reorder = (unit[:, None] == source[None, :]).astype(jnp.bfloat16)
    dz_ordered = jnp.dot(dz_in, reorder, preferred_element_type=jnp.float32).astype(jnp.bfloat16)
    partial = dot_t(dz_ordered, x_in).astype(jnp.bfloat16)
    summed = lax.psum_scatter(partial, "z", scatter_dimension=0, tiled=True)

    matrix = weight[0]
    row_grads = lax.dot_general(
        dz_in, matrix, (((1,), (1,)), ((), ())), preferred_element_type=jnp.float32
    ).astype(jnp.bfloat16)
    z = jnp.dot(x_in, matrix, preferred_element_type=jnp.float32)
    terms = jnp.sum(dz_in.astype(jnp.float32) * z, axis=1).astype(jnp.bfloat16)
    reply = jnp.concatenate(
        [
            row_grads.reshape(experts, x_lines, LANE),
            jnp.pad(terms.reshape(experts, 1, CAP), ((0, 0), (0, 15), (0, LANE - CAP))),
        ],
        axis=1,
    )
    back = lax.all_to_all(reply, EXPERT_AXES, 0, 0, tiled=True)

    side = lax.axis_index("xh")
    keep = lax.dynamic_slice_in_dim(summed, side * shard, shard, 0)
    give = lax.dynamic_slice_in_dim(summed, (1 - side) * shard, shard, 0)
    got = lax.ppermute(give, "xh", [(0, 1), (1, 0)])
    weight_grads = keep.astype(jnp.float32) + got.astype(jnp.float32)

    back_rows = back[:, :x_lines].reshape(slots, width)
    back_terms = back[:, x_lines, :CAP].reshape(slots).astype(jnp.float32)
    token_grads = jnp.dot(token_place, back_rows, preferred_element_type=jnp.float32).astype(
        jnp.bfloat16
    )
    picked = jnp.sum(jnp.where(placing, back_terms[None, :], 0.0), axis=1)
    gate_grads = (picked.reshape(toks, picks) / gate_values.astype(jnp.float32)).astype(
        jnp.bfloat16
    )
    return token_grads, gate_grads, weight_grads.T[None]


def solution(mesh):
    n_dp, n_expert = mesh.shape["dp"], mesh.shape["expert"]
    fine = Mesh(mesh.devices.reshape(2, n_dp // 2, n_expert // 4, 2, 2), ALL_AXES)
    rows = P(ALL_AXES)
    in_specs = (rows, rows, rows, rows, rows, P(EXPERT_AXES))
    out_specs = (rows, rows, P(EXPERT_AXES, None, ("xh", "z")))
    return jax.shard_map(
        local, mesh=fine, in_specs=in_specs, out_specs=out_specs, check_vma=False
    )
```

```python
import jax
import jax.numpy as jnp
from jax import lax
from jax.experimental import pallas as pl
from jax.experimental.pallas import tpu as pltpu
from jax.sharding import Mesh, PartitionSpec as P

CAP = 5
LANE = 128
EXPERT_AXES = ("y", "xl", "c")
ALL_AXES = ("xh", "z") + EXPERT_AXES


def dot_t(a, b):
    return lax.dot_general(a, b, (((0,), (0,)), ((), ())), preferred_element_type=jnp.float32)


def partial_kernel(x_ref, dz_ref, order_ref, out_ref, dz_t):
    @pl.when(pl.program_id(0) == 0)
    def _():
        dz_t[...] = lax.dot_general(
            order_ref[...], dz_ref[...], (((0,), (1,)), ((), ())), preferred_element_type=jnp.float32
        ).astype(jnp.bfloat16)

    out_ref[...] = jnp.dot(
        dz_t[...], x_ref[...], preferred_element_type=jnp.float32
    ).astype(jnp.bfloat16)


def partial_of(x, dz, order, block=512):
    rows, width = x.shape
    hidden = dz.shape[1]
    return pl.pallas_call(
        partial_kernel,
        grid=(width // block,),
        in_specs=[
            pl.BlockSpec((rows, block), lambda i: (0, i)),
            pl.BlockSpec((rows, hidden), lambda i: (0, 0)),
            pl.BlockSpec((hidden, hidden), lambda i: (0, 0)),
        ],
        out_specs=pl.BlockSpec((hidden, block), lambda i: (0, i)),
        out_shape=jax.ShapeDtypeStruct((hidden, width), jnp.bfloat16),
        scratch_shapes=[pltpu.VMEM((hidden, rows), jnp.bfloat16)],
        compiler_params=pltpu.CompilerParams(vmem_limit_bytes=16 * 1024 * 1024),
        cost_estimate=pl.CostEstimate(
            flops=2 * rows * hidden * (width + hidden),
            bytes_accessed=2 * (hidden * width + rows * width + hidden * hidden),
            transcendentals=0,
        ),
    )(x, dz, order)


def local(token_rows, row_scales, expert_ids, gate_values, upstream, weight):
    toks, picks = expert_ids.shape
    width = token_rows.shape[1]
    hidden = upstream.shape[2]
    experts = lax.axis_size(EXPERT_AXES)
    depth = lax.axis_size("z")
    slots = experts * CAP
    choices = toks * picks
    half = hidden // 2
    x_lines = CAP * width // LANE
    dz_lines = CAP * hidden // LANE

    x = (row_scales.astype(jnp.float32)[:, None] * token_rows.astype(jnp.float32)).astype(
        jnp.bfloat16
    )
    dz = (gate_values.astype(jnp.float32)[..., None] * upstream.astype(jnp.float32)).astype(
        jnp.bfloat16
    )
    column = jnp.arange(slots, dtype=jnp.int32)
    named = expert_ids[:, :, None] == (column // CAP)[None, None, :]
    names = jnp.any(named, axis=1)
    row = jnp.arange(toks, dtype=jnp.int32)
    earlier = (row[None, :] < row[:, None]).astype(jnp.bfloat16)
    rank = jnp.dot(earlier, names.astype(jnp.bfloat16), preferred_element_type=jnp.float32)
    token_placing = names & (rank == (column % CAP).astype(jnp.float32)[None, :])
    token_place = token_placing.astype(jnp.bfloat16)
    placing = (named & token_placing[:, None, :]).reshape(choices, slots)
    place = placing.astype(jnp.bfloat16)

    send_x = dot_t(token_place, x).astype(jnp.bfloat16)
    send_dz = dot_t(place, dz.reshape(choices, hidden)).astype(jnp.bfloat16)
    pad = width // LANE - dz_lines
    message = jnp.concatenate(
        [
            send_x.reshape(experts, x_lines, LANE),
            send_dz.reshape(experts, dz_lines, LANE),
            jnp.zeros((experts, pad, LANE), jnp.bfloat16),
        ],
        axis=1,
    )
    mine = lax.all_to_all(message, EXPERT_AXES, 0, 0, tiled=True)
    x_in = mine.reshape(experts * (CAP + 1), width)
    dz_in = mine[:, x_lines : x_lines + dz_lines].reshape(slots, hidden)
    dz_six = jnp.pad(dz_in.reshape(experts, CAP, hidden), ((0, 0), (0, 1), (0, 0))).reshape(
        experts * (CAP + 1), hidden
    )

    unit = jnp.arange(hidden)
    shard = hidden // (2 * depth)
    source = (unit // shard % 2) * half + unit // (2 * shard) * shard + unit % shard
    reorder = (unit[:, None] == source[None, :]).astype(jnp.bfloat16)
    partial = partial_of(x_in, dz_six, reorder)
    summed = lax.psum_scatter(partial, "z", scatter_dimension=0, tiled=True)

    matrix = weight[0]
    row_grads = lax.dot_general(
        dz_in, matrix, (((1,), (1,)), ((), ())), preferred_element_type=jnp.float32
    ).astype(jnp.bfloat16)
    z = jnp.dot(x_in, matrix, preferred_element_type=jnp.float32)
    terms = jnp.sum(dz_six.astype(jnp.float32) * z, axis=1).astype(jnp.bfloat16)
    terms = terms.reshape(experts, CAP + 1)[:, :CAP]
    reply = jnp.concatenate(
        [
            row_grads.reshape(experts, x_lines, LANE),
            jnp.pad(terms.reshape(experts, 1, CAP), ((0, 0), (0, 15), (0, LANE - CAP))),
        ],
        axis=1,
    )
    back = lax.all_to_all(reply, EXPERT_AXES, 0, 0, tiled=True)

    side = lax.axis_index("xh")
    keep = lax.dynamic_slice_in_dim(summed, side * shard, shard, 0)
    give = lax.dynamic_slice_in_dim(summed, (1 - side) * shard, shard, 0)
    got = lax.ppermute(give, "xh", [(0, 1), (1, 0)])
    weight_grads = keep.astype(jnp.float32) + got.astype(jnp.float32)

    back_rows = back[:, :x_lines].reshape(slots, width)
    back_terms = back[:, x_lines, :CAP].reshape(slots).astype(jnp.float32)
    token_grads = jnp.dot(token_place, back_rows, preferred_element_type=jnp.float32).astype(
        jnp.bfloat16
    )
    picked = jnp.sum(jnp.where(placing, back_terms[None, :], 0.0), axis=1)
    gate_grads = (picked.reshape(toks, picks) / gate_values.astype(jnp.float32)).astype(
        jnp.bfloat16
    )
    return token_grads, gate_grads, weight_grads.T[None]


def solution(mesh):
    n_dp, n_expert = mesh.shape["dp"], mesh.shape["expert"]
    fine = Mesh(mesh.devices.reshape(2, n_dp // 2, n_expert // 4, 2, 2), ALL_AXES)
    rows = P(ALL_AXES)
    in_specs = (rows, rows, rows, rows, rows, P(EXPERT_AXES))
    out_specs = (rows, rows, P(EXPERT_AXES, None, ("xh", "z")))
    return jax.shard_map(
        local, mesh=fine, in_specs=in_specs, out_specs=out_specs, check_vma=False
    )
```

```python
import jax
import jax.numpy as jnp
from jax import lax
from jax.experimental import pallas as pl
from jax.experimental.pallas import tpu as pltpu
from jax.sharding import Mesh, PartitionSpec as P

CAP = 5
LANE = 128
EXPERT_AXES = ("y", "xl", "c")
ALL_AXES = ("xh", "z") + EXPERT_AXES


def dot_t(a, b):
    return lax.dot_general(a, b, (((0,), (0,)), ((), ())), preferred_element_type=jnp.float32)


def partial_kernel(x_ref, dz_ref, order_ref, spread_ref, out_ref, dz_t):
    @pl.when(pl.program_id(0) == 0)
    def _():
        ordered = jnp.dot(dz_ref[...], order_ref[...], preferred_element_type=jnp.float32)
        dz_t[...] = dot_t(ordered.astype(jnp.bfloat16), spread_ref[...]).astype(jnp.bfloat16)

    out_ref[...] = jnp.dot(
        dz_t[...], x_ref[...], preferred_element_type=jnp.float32
    ).astype(jnp.bfloat16)


def partial_of(x, dz, order, spread, block=512):
    rows, width = x.shape
    slots, hidden = dz.shape
    return pl.pallas_call(
        partial_kernel,
        grid=(width // block,),
        in_specs=[
            pl.BlockSpec((rows, block), lambda i: (0, i)),
            pl.BlockSpec((slots, hidden), lambda i: (0, 0)),
            pl.BlockSpec((hidden, hidden), lambda i: (0, 0)),
            pl.BlockSpec((slots, rows), lambda i: (0, 0)),
        ],
        out_specs=pl.BlockSpec((hidden, block), lambda i: (0, i)),
        out_shape=pltpu.HBM((hidden, width), jnp.bfloat16),
        scratch_shapes=[pltpu.VMEM((hidden, rows), jnp.bfloat16)],
        compiler_params=pltpu.CompilerParams(vmem_limit_bytes=16 * 1024 * 1024),
        cost_estimate=pl.CostEstimate(
            flops=2 * rows * hidden * (width + hidden),
            bytes_accessed=2 * (hidden * width + rows * width + hidden * hidden),
            transcendentals=0,
        ),
    )(x, dz, order, spread)


def local(token_rows, row_scales, expert_ids, gate_values, upstream, weight):
    toks, picks = expert_ids.shape
    width = token_rows.shape[1]
    hidden = upstream.shape[2]
    experts = lax.axis_size(EXPERT_AXES)
    depth = lax.axis_size("z")
    slots = experts * CAP
    choices = toks * picks
    half = hidden // 2
    x_lines = CAP * width // LANE
    dz_lines = CAP * hidden // LANE

    x = (row_scales.astype(jnp.float32)[:, None] * token_rows.astype(jnp.float32)).astype(
        jnp.bfloat16
    )
    dz = (gate_values.astype(jnp.float32)[..., None] * upstream.astype(jnp.float32)).astype(
        jnp.bfloat16
    )
    column = jnp.arange(slots, dtype=jnp.int32)
    named = expert_ids[:, :, None] == (column // CAP)[None, None, :]
    names = jnp.any(named, axis=1)
    row = jnp.arange(toks, dtype=jnp.int32)
    earlier = (row[None, :] < row[:, None]).astype(jnp.bfloat16)
    rank = jnp.dot(earlier, names.astype(jnp.bfloat16), preferred_element_type=jnp.float32)
    token_placing = names & (rank == (column % CAP).astype(jnp.float32)[None, :])
    token_place = token_placing.astype(jnp.bfloat16)
    placing = (named & token_placing[:, None, :]).reshape(choices, slots)
    place = placing.astype(jnp.bfloat16)

    send_x = dot_t(token_place, x).astype(jnp.bfloat16)
    send_dz = dot_t(place, dz.reshape(choices, hidden)).astype(jnp.bfloat16)
    pad = width // LANE - dz_lines
    message = jnp.concatenate(
        [
            send_x.reshape(experts, x_lines, LANE),
            send_dz.reshape(experts, dz_lines, LANE),
            jnp.zeros((experts, pad, LANE), jnp.bfloat16),
        ],
        axis=1,
    )
    mine = lax.all_to_all(message, EXPERT_AXES, 0, 0, tiled=True)
    x_in = mine.reshape(experts * (CAP + 1), width)
    dz_in = mine[:, x_lines : x_lines + dz_lines].reshape(slots, hidden)

    unit = jnp.arange(hidden)
    shard = hidden // (2 * depth)
    source = (unit // shard % 2) * half + unit // (2 * shard) * shard + unit % shard
    reorder = (unit[:, None] == source[None, :]).astype(jnp.bfloat16)
    six = jnp.arange(experts * (CAP + 1))
    spread = (column + column // CAP)[:, None] == six[None, :]
    partial = partial_of(x_in, dz_in, reorder, spread.astype(jnp.bfloat16))
    summed = lax.psum_scatter(partial, "z", scatter_dimension=0, tiled=True)

    matrix = weight[0]
    row_grads = lax.dot_general(
        dz_in, matrix, (((1,), (1,)), ((), ())), preferred_element_type=jnp.float32
    ).astype(jnp.bfloat16)
    z = jnp.dot(x_in, matrix, preferred_element_type=jnp.float32)
    z = z.reshape(experts, CAP + 1, hidden)[:, :CAP].reshape(slots, hidden)
    terms = jnp.sum(dz_in.astype(jnp.float32) * z, axis=1).astype(jnp.bfloat16)
    reply = jnp.concatenate(
        [
            row_grads.reshape(experts, x_lines, LANE),
            jnp.pad(terms.reshape(experts, 1, CAP), ((0, 0), (0, 15), (0, LANE - CAP))),
        ],
        axis=1,
    )
    back = lax.all_to_all(reply, EXPERT_AXES, 0, 0, tiled=True)

    side = lax.axis_index("xh")
    keep = lax.dynamic_slice_in_dim(summed, side * shard, shard, 0)
    give = lax.dynamic_slice_in_dim(summed, (1 - side) * shard, shard, 0)
    got = lax.ppermute(give, "xh", [(0, 1), (1, 0)])
    weight_grads = keep.astype(jnp.float32) + got.astype(jnp.float32)

    back_rows = back[:, :x_lines].reshape(slots, width)
    back_terms = back[:, x_lines, :CAP].reshape(slots).astype(jnp.float32)
    token_grads = jnp.dot(token_place, back_rows, preferred_element_type=jnp.float32).astype(
        jnp.bfloat16
    )
    picked = jnp.sum(jnp.where(placing, back_terms[None, :], 0.0), axis=1)
    gate_grads = (picked.reshape(toks, picks) / gate_values.astype(jnp.float32)).astype(
        jnp.bfloat16
    )
    return token_grads, gate_grads, weight_grads.T[None]


def solution(mesh):
    n_dp, n_expert = mesh.shape["dp"], mesh.shape["expert"]
    fine = Mesh(mesh.devices.reshape(2, n_dp // 2, n_expert // 4, 2, 2), ALL_AXES)
    rows = P(ALL_AXES)
    in_specs = (rows, rows, rows, rows, rows, P(EXPERT_AXES))
    out_specs = (rows, rows, P(EXPERT_AXES, None, ("xh", "z")))
    return jax.shard_map(
        local, mesh=fine, in_specs=in_specs, out_specs=out_specs, check_vma=False
    )
```

```python
import jax
import jax.numpy as jnp
from jax import lax
from jax.sharding import Mesh, PartitionSpec as P

CAP = 5
LANE = 128
EXPERT_AXES = ("y", "xl", "c")
ALL_AXES = ("xh", "z") + EXPERT_AXES


def dot_t(a, b):
    return lax.dot_general(a, b, (((0,), (0,)), ((), ())), preferred_element_type=jnp.float32)


def local(token_rows, row_scales, expert_ids, gate_values, upstream, weight):
    toks, picks = expert_ids.shape
    width = token_rows.shape[1]
    hidden = upstream.shape[2]
    experts = lax.axis_size(EXPERT_AXES)
    depth = lax.axis_size("z")
    slots = experts * CAP
    choices = toks * picks
    half = hidden // 2
    x_lines = CAP * width // LANE
    dz_lines = CAP * hidden // LANE

    x = (row_scales.astype(jnp.float32)[:, None] * token_rows.astype(jnp.float32)).astype(
        jnp.bfloat16
    )
    dz = (gate_values.astype(jnp.float32)[..., None] * upstream.astype(jnp.float32)).astype(
        jnp.bfloat16
    )
    column = jnp.arange(slots, dtype=jnp.int32)
    named = expert_ids[:, :, None] == (column // CAP)[None, None, :]
    names = jnp.any(named, axis=1)
    row = jnp.arange(toks, dtype=jnp.int32)
    earlier = (row[None, :] < row[:, None]).astype(jnp.bfloat16)
    rank = jnp.dot(earlier, names.astype(jnp.bfloat16), preferred_element_type=jnp.float32)
    token_placing = names & (rank == (column % CAP).astype(jnp.float32)[None, :])
    token_place = token_placing.astype(jnp.bfloat16)
    placing = (named & token_placing[:, None, :]).reshape(choices, slots)
    place = placing.astype(jnp.bfloat16)

    send_x = dot_t(token_place, x).astype(jnp.bfloat16)
    send_dz = dot_t(place, dz.reshape(choices, hidden)).astype(jnp.bfloat16)
    pad = (-(x_lines + dz_lines)) % 16
    message = jnp.concatenate(
        [
            send_x.reshape(experts, x_lines, LANE),
            send_dz.reshape(experts, dz_lines, LANE),
            jnp.zeros((experts, pad, LANE), jnp.bfloat16),
        ],
        axis=1,
    )
    mine = lax.all_to_all(message, EXPERT_AXES, 0, 0, tiled=True)
    x_in = mine[:, :x_lines].reshape(slots, width)
    dz_in = mine[:, x_lines : x_lines + dz_lines].reshape(slots, hidden)

    unit = jnp.arange(hidden)
    shard = hidden // (2 * depth)
    source = (unit // shard % 2) * half + unit // (2 * shard) * shard + unit % shard
    reorder = (unit[:, None] == source[None, :]).astype(jnp.bfloat16)
    dz_ordered = jnp.dot(dz_in, reorder, preferred_element_type=jnp.float32).astype(jnp.bfloat16)
    partial = dot_t(dz_ordered, x_in).astype(jnp.bfloat16)
    summed = lax.psum_scatter(partial, "z", scatter_dimension=0, tiled=True)

    matrix = weight[0]
    row_grads = lax.dot_general(
        dz_in, matrix, (((1,), (1,)), ((), ())), preferred_element_type=jnp.float32
    ).astype(jnp.bfloat16)
    z = jnp.dot(x_in, matrix, preferred_element_type=jnp.float32)
    terms = jnp.sum(dz_in.astype(jnp.float32) * z, axis=1).astype(jnp.bfloat16)
    reply = jnp.concatenate(
        [
            row_grads.reshape(experts, x_lines, LANE),
            jnp.pad(terms.reshape(experts, 1, CAP), ((0, 0), (0, 15), (0, LANE - CAP))),
        ],
        axis=1,
    )
    back = lax.all_to_all(reply, EXPERT_AXES, 0, 0, tiled=True)

    side = lax.axis_index("xh")
    keep = lax.dynamic_slice_in_dim(summed, side * shard, shard, 0)
    give = lax.dynamic_slice_in_dim(summed, (1 - side) * shard, shard, 0)
    got = lax.ppermute(give, "xh", [(0, 1), (1, 0)])
    weight_grads = keep.astype(jnp.float32) + got.astype(jnp.float32)

    back_rows = back[:, :x_lines].reshape(slots, width)
    back_terms = back[:, x_lines, :CAP].reshape(slots).astype(jnp.float32)
    token_grads = jnp.dot(token_place, back_rows, preferred_element_type=jnp.float32).astype(
        jnp.bfloat16
    )
    picked = jnp.sum(jnp.where(placing, back_terms[None, :], 0.0), axis=1)
    gate_grads = (picked.reshape(toks, picks) / gate_values.astype(jnp.float32)).astype(
        jnp.bfloat16
    )
    return token_grads, gate_grads, weight_grads.T[None]


def solution(mesh):
    n_dp, n_expert = mesh.shape["dp"], mesh.shape["expert"]
    fine = Mesh(mesh.devices.reshape(2, n_dp // 2, n_expert // 4, 2, 2), ALL_AXES)
    rows = P(ALL_AXES)
    in_specs = (rows, rows, rows, rows, rows, P(EXPERT_AXES))
    out_specs = (rows, rows, P(EXPERT_AXES, None, ("xh", "z")))
    return jax.shard_map(
        local, mesh=fine, in_specs=in_specs, out_specs=out_specs, check_vma=False
    )
```

```python
import jax
import jax.numpy as jnp
from jax import lax
from jax.sharding import Mesh, PartitionSpec as P

CAP = 5
LANE = 128
EXPERT_AXES = ("y", "xl", "c")
ALL_AXES = ("xh", "z") + EXPERT_AXES


def dot_t(a, b):
    return lax.dot_general(a, b, (((0,), (0,)), ((), ())), preferred_element_type=jnp.float32)


def local(token_rows, row_scales, expert_ids, gate_values, upstream, weight):
    toks, picks = expert_ids.shape
    width = token_rows.shape[1]
    hidden = upstream.shape[2]
    experts = lax.axis_size(EXPERT_AXES)
    slots = experts * CAP
    choices = toks * picks
    half = hidden // 2
    x_lines = CAP * width // LANE
    dz_lines = CAP * hidden // LANE

    x = (row_scales.astype(jnp.float32)[:, None] * token_rows.astype(jnp.float32)).astype(
        jnp.bfloat16
    )
    dz = (gate_values.astype(jnp.float32)[..., None] * upstream.astype(jnp.float32)).astype(
        jnp.bfloat16
    )
    column = jnp.arange(slots, dtype=jnp.int32)
    named = expert_ids[:, :, None] == (column // CAP)[None, None, :]
    names = jnp.any(named, axis=1)
    row = jnp.arange(toks, dtype=jnp.int32)
    earlier = (row[None, :] < row[:, None]).astype(jnp.bfloat16)
    rank = jnp.dot(earlier, names.astype(jnp.bfloat16), preferred_element_type=jnp.float32)
    token_placing = names & (rank == (column % CAP).astype(jnp.float32)[None, :])
    token_place = token_placing.astype(jnp.bfloat16)
    placing = (named & token_placing[:, None, :]).reshape(choices, slots)
    place = placing.astype(jnp.bfloat16)

    send_x = dot_t(token_place, x).astype(jnp.bfloat16)
    send_dz = dot_t(place, dz.reshape(choices, hidden)).astype(jnp.bfloat16)
    cut = width // 2
    cut_lines = x_lines // 2
    pad = (-(cut_lines + dz_lines)) % 16
    first = jnp.concatenate(
        [
            send_x[:, :cut].reshape(experts, cut_lines, LANE),
            send_dz.reshape(experts, dz_lines, LANE),
            jnp.zeros((experts, pad, LANE), jnp.bfloat16),
        ],
        axis=1,
    )
    second = send_x[:, cut:].reshape(experts, cut_lines, LANE)
    swap = [(0, 1), (1, 0)]
    mine = lax.all_to_all(first, EXPERT_AXES, 0, 0, tiled=True)
    mine, second = lax.optimization_barrier((mine, second))
    other = lax.ppermute(mine, "xh", swap)
    mine_late = lax.all_to_all(second, EXPERT_AXES, 0, 0, tiled=True)
    other_late = lax.ppermute(mine_late, "xh", swap)

    def unpack(early, late):
        rows = jnp.concatenate(
            [early[:, :cut_lines].reshape(slots, cut), late.reshape(slots, cut)], axis=1
        )
        return rows, early[:, cut_lines : cut_lines + dz_lines].reshape(slots, hidden)

    x_in, dz_in = unpack(mine, mine_late)
    x_other, dz_other = unpack(other, other_late)
    at = lax.axis_index("xh") * half
    dz_both = jnp.concatenate(
        [
            lax.dynamic_slice_in_dim(dz_in, at, half, 1),
            lax.dynamic_slice_in_dim(dz_other, at, half, 1),
        ],
        axis=0,
    )
    partial = dot_t(dz_both, jnp.concatenate([x_in, x_other], axis=0)).astype(jnp.bfloat16)
    weight_grads = lax.psum_scatter(partial, "z", scatter_dimension=0, tiled=True)

    matrix = weight[0]
    row_grads = lax.dot_general(
        dz_in, matrix, (((1,), (1,)), ((), ())), preferred_element_type=jnp.float32
    ).astype(jnp.bfloat16)
    z = jnp.dot(x_in, matrix, preferred_element_type=jnp.float32)
    terms = jnp.sum(dz_in.astype(jnp.float32) * z, axis=1).astype(jnp.bfloat16)
    reply = jnp.concatenate(
        [
            row_grads.reshape(experts, x_lines, LANE),
            jnp.pad(terms.reshape(experts, 1, CAP), ((0, 0), (0, 15), (0, LANE - CAP))),
        ],
        axis=1,
    )
    back = lax.all_to_all(reply, EXPERT_AXES, 0, 0, tiled=True)

    back_rows = back[:, :x_lines].reshape(slots, width)
    back_terms = back[:, x_lines, :CAP].reshape(slots).astype(jnp.float32)
    token_grads = jnp.dot(token_place, back_rows, preferred_element_type=jnp.float32).astype(
        jnp.bfloat16
    )
    picked = jnp.sum(jnp.where(placing, back_terms[None, :], 0.0), axis=1)
    gate_grads = (picked.reshape(toks, picks) / gate_values.astype(jnp.float32)).astype(
        jnp.bfloat16
    )
    return token_grads, gate_grads, weight_grads.astype(jnp.float32).T[None]


def solution(mesh):
    n_dp, n_expert = mesh.shape["dp"], mesh.shape["expert"]
    fine = Mesh(mesh.devices.reshape(2, n_dp // 2, n_expert // 4, 2, 2), ALL_AXES)
    rows = P(ALL_AXES)
    in_specs = (rows, rows, rows, rows, rows, P(EXPERT_AXES))
    out_specs = (rows, rows, P(EXPERT_AXES, None, ("xh", "z")))
    return jax.shard_map(
        local, mesh=fine, in_specs=in_specs, out_specs=out_specs, check_vma=False
    )
```

```python
import jax
import jax.numpy as jnp
from jax import lax
from jax.sharding import Mesh, PartitionSpec as P

CAP = 5
LANE = 128
EXPERT_AXES = ("y", "xl", "c")
ALL_AXES = ("xh", "z") + EXPERT_AXES


def dot_t(a, b):
    return lax.dot_general(a, b, (((0,), (0,)), ((), ())), preferred_element_type=jnp.float32)


def local(token_rows, row_scales, expert_ids, gate_values, upstream, weight):
    toks, picks = expert_ids.shape
    width = token_rows.shape[1]
    hidden = upstream.shape[2]
    experts = lax.axis_size(EXPERT_AXES)
    depth = lax.axis_size("z")
    slots = experts * CAP
    choices = toks * picks
    half = hidden // 2
    x_lines = CAP * width // LANE
    dz_lines = CAP * hidden // LANE

    column = jnp.arange(slots, dtype=jnp.int32)
    named = expert_ids[:, :, None] == (column // CAP)[None, None, :]
    names = jnp.any(named, axis=1)
    row = jnp.arange(toks, dtype=jnp.int32)
    earlier = (row[None, :] < row[:, None]).astype(jnp.bfloat16)
    rank = jnp.dot(earlier, names.astype(jnp.bfloat16), preferred_element_type=jnp.float32)
    token_placing = names & (rank == (column % CAP).astype(jnp.float32)[None, :])
    token_place = token_placing.astype(jnp.bfloat16)
    placing = (named & token_placing[:, None, :]).reshape(choices, slots)

    scaled_place = jnp.where(token_placing, row_scales[:, None], 0)
    gated_place = jnp.where(placing, gate_values.reshape(choices, 1), 0)
    send_x = dot_t(scaled_place, token_rows).astype(jnp.bfloat16)
    send_dz = dot_t(gated_place, upstream.reshape(choices, hidden)).astype(jnp.bfloat16)
    pad = (-(x_lines + dz_lines)) % 16
    message = jnp.concatenate(
        [
            send_x.reshape(experts, x_lines, LANE),
            send_dz.reshape(experts, dz_lines, LANE),
            jnp.zeros((experts, pad, LANE), jnp.bfloat16),
        ],
        axis=1,
    )
    mine = lax.all_to_all(message, EXPERT_AXES, 0, 0, tiled=True)
    x_in = mine[:, :x_lines].reshape(slots, width)
    dz_in = mine[:, x_lines : x_lines + dz_lines].reshape(slots, hidden)

    unit = jnp.arange(hidden)
    shard = hidden // (2 * depth)
    source = (unit // shard % 2) * half + unit // (2 * shard) * shard + unit % shard
    reorder = (unit[:, None] == source[None, :]).astype(jnp.bfloat16)
    dz_ordered = jnp.dot(dz_in, reorder, preferred_element_type=jnp.float32).astype(jnp.bfloat16)
    partial = dot_t(dz_ordered, x_in).astype(jnp.bfloat16)
    summed = lax.psum_scatter(partial, "z", scatter_dimension=0, tiled=True)

    matrix = weight[0]
    row_grads = lax.dot_general(
        dz_in, matrix, (((1,), (1,)), ((), ())), preferred_element_type=jnp.float32
    ).astype(jnp.bfloat16)
    z = jnp.dot(x_in, matrix, preferred_element_type=jnp.float32)
    terms = jnp.sum(dz_in.astype(jnp.float32) * z, axis=1).astype(jnp.bfloat16)
    reply = jnp.concatenate(
        [
            row_grads.reshape(experts, x_lines, LANE),
            jnp.pad(terms.reshape(experts, 1, CAP), ((0, 0), (0, 15), (0, LANE - CAP))),
        ],
        axis=1,
    )
    back = lax.all_to_all(reply, EXPERT_AXES, 0, 0, tiled=True)

    side = lax.axis_index("xh")
    keep = lax.dynamic_slice_in_dim(summed, side * shard, shard, 0)
    give = lax.dynamic_slice_in_dim(summed, (1 - side) * shard, shard, 0)
    got = lax.ppermute(give, "xh", [(0, 1), (1, 0)])
    weight_grads = keep.astype(jnp.float32) + got.astype(jnp.float32)

    back_rows = back[:, :x_lines].reshape(slots, width)
    back_terms = back[:, x_lines, :CAP].reshape(slots).astype(jnp.float32)
    token_grads = jnp.dot(token_place, back_rows, preferred_element_type=jnp.float32).astype(
        jnp.bfloat16
    )
    picked = jnp.sum(jnp.where(placing, back_terms[None, :], 0.0), axis=1)
    gate_grads = (picked.reshape(toks, picks) / gate_values.astype(jnp.float32)).astype(
        jnp.bfloat16
    )
    return token_grads, gate_grads, weight_grads.T[None]


def solution(mesh):
    n_dp, n_expert = mesh.shape["dp"], mesh.shape["expert"]
    fine = Mesh(mesh.devices.reshape(2, n_dp // 2, n_expert // 4, 2, 2), ALL_AXES)
    rows = P(ALL_AXES)
    in_specs = (rows, rows, rows, rows, rows, P(EXPERT_AXES))
    out_specs = (rows, rows, P(EXPERT_AXES, None, ("xh", "z")))
    return jax.shard_map(
        local, mesh=fine, in_specs=in_specs, out_specs=out_specs, check_vma=False
    )
```
